32 devices in a mesh: groups: 2 (over x), rows: 16 (over z, y, core).
Axes of the slice: x: 2, y: 2, z: 4, core: 2. Of those that a mesh axis runs over, the one named last changes fastest.
Arguments:
- a_blocks: bfloat16 [256, 8, 256, 256], P(('groups', 'rows')), parts along dimension 0, may hold values from -8 to 8
- basis_in: bfloat16 [65536, 128], P(('groups', 'rows')), parts along dimension 0, may hold values from -5 to 5
- pattern: int32 [256, 8], P(('groups', 'rows')), parts along dimension 0, may hold values from 0 to 127, as said below
Outputs:
- basis_out: float32 [65536, 128], P(('groups', 'rows')), parts along dimension 0
- factor: float32 [256, 128], P('groups'), parts along dimension 0
The draws below stay inside these ranges and needn't reach their ends.
There are 2 independent parts, one for each index of `groups`. The reference program is written for one: setup_inputs(seed, part) draws one part's arguments, and reference() takes and returns one part's arrays. A program takes and returns all parts, laid end to end along the dimension named above; each array names one. Nothing has to cross between parts.
Inputs may be any that keep to these rules, and one draw needn't show every extreme that they name: `pattern`: the 64 entries of the block rows of one device name blocks of at most 15 other devices; those naming blocks of any one other device number at most 5 and name at most 1 distinct blocks; all three bounds are reached in every draw. The entries of one block row that name blocks of other devices are distinct.
All inputs are finite; a program needn't handle non-finite values.
Results may differ from the reference program's by a relative error of at most 0.0003.
Values may be sent and summed in bfloat16 or wider, within the bound.
A program may use at most 128 MiB of HBM per device.

```python
import math
import jax
import jax.numpy as jnp
from jax import lax

K = 128
B = 256
NNZ = 8
BR_DEV = 8
NBR = 128
NODES = 32768
N_ROWS = 16


def draw_a_blocks(key, part):
    key_base, key_rows, key_cols = jax.random.split(key, 3)
    base = jnp.clip(jax.random.normal(key_base, (NBR, NNZ, B, B), jnp.float32), -6.0, 6.0)
    row_log = jax.random.uniform(key_rows, (NBR, 1, B, 1), jnp.float32, 0.0, math.log(10.0))
    col_log = jax.random.uniform(key_cols, (NBR, NNZ, 1, B), jnp.float32, 0.0, math.log(10.0)) - 0.5 * math.log(10.0)
    rising = jnp.arange(NBR, dtype=jnp.float32).reshape(NBR, 1, 1, 1) * (math.log(3.0) / NBR)
    scale_all = jnp.exp(row_log + col_log + rising - 0.5 * math.log(10.0)) / math.sqrt(NNZ * B)
    return (base * scale_all).astype(jnp.bfloat16)


def draw_basis_in(key, part):
    key_base = jax.random.fold_in(key, 0)
    values = jnp.clip(jax.random.normal(key_base, (NODES, K), jnp.float32), -5.0, 5.0)
    return values.astype(jnp.bfloat16)


def draw_pattern(key, part):
    ref_count = BR_DEV * NNZ
    owner_count = min(ref_count - 1, N_ROWS - 1)
    key_devices, key_forced = jax.random.split(jax.random.fold_in(key, 11), 2)

    def one_device(device_key, device):
        key_perm, key_block, key_local, key_level, key_far = jax.random.split(device_key, 5)
        offsets = jax.random.permutation(key_perm, N_ROWS - 1)[:owner_count] + 1
        owners = (device + offsets) % N_ROWS
        owner_blocks = jax.random.randint(key_block, (owner_count,), 0, BR_DEV)
        residue = jnp.arange(ref_count, dtype=jnp.int32) % owner_count
        far_cols = owners[residue] * BR_DEV + owner_blocks[residue]
        local_cols = device * BR_DEV + jax.random.randint(key_local, (ref_count,), 0, BR_DEV)
        far_level = jax.random.randint(key_level, (), 3, 5)
        far_mask = jax.random.randint(key_far, (ref_count,), 0, 4) < far_level
        return (far_cols, local_cols, far_mask)
    device_keys = jax.random.split(key_devices, N_ROWS)
    devices = jnp.arange(N_ROWS, dtype=jnp.int32)
    far_cols, local_cols, far_mask = jax.vmap(one_device)(device_keys, devices)
    forced = jax.random.randint(key_forced, (), 0, N_ROWS)
    far_mask = far_mask | (devices[:, None] == forced)
    chosen = jnp.where(far_mask, far_cols, local_cols)
    return chosen.reshape(NBR, NNZ).astype(jnp.int32)


def setup_inputs(seed: int = 0, part: int = 0) -> dict:
    arg_keys = jax.random.split(jax.random.key(seed), 4)
    own_keys = jax.random.split(jax.random.fold_in(arg_keys[3], part), 4)
    return {
        "a_blocks": draw_a_blocks(jax.random.fold_in(jax.random.fold_in(arg_keys[3], part), 71), part),
        "basis_in": draw_basis_in(jax.random.fold_in(jax.random.fold_in(arg_keys[3], part), 71), part),
        "pattern": draw_pattern(jax.random.fold_in(jax.random.fold_in(arg_keys[3], part), 71), part),
    }


def reference(a_blocks, basis_in, pattern):
    block_rows, slot_count, block_size, unused = a_blocks.shape
    columns = basis_in.shape[1]
    blocks = basis_in.reshape(block_rows, block_size, columns)
    groups = block_rows // BR_DEV

    def one_group(group_item):
        group_blocks, group_cols = group_item
        operand = jnp.take(blocks, group_cols, axis=0).astype(jnp.float32)
        return jnp.einsum('rsij,rsjk->rik', group_blocks.astype(jnp.float32), operand, precision=lax.Precision.HIGHEST)
    image = lax.map(one_group, (a_blocks.reshape(groups, BR_DEV, slot_count, block_size, block_size), pattern.reshape(groups, BR_DEV, slot_count)))
    image = image.reshape(block_rows * block_size, columns)
    gram = jnp.einsum('nk,nl->kl', image, image, precision=lax.Precision.HIGHEST) / (block_rows * block_size)
    factor = jnp.linalg.cholesky(gram).T
    basis_out = lax.linalg.triangular_solve(factor, image, left_side=False, lower=False)
    return (basis_out, factor)
```

```python
import functools
import jax
import jax.numpy as jnp
from jax import lax
from jax.experimental import pallas as pl
from jax.experimental.pallas import tpu as pltpu
from jax.sharding import PartitionSpec as P

MESH = pl.DeviceIdType.MESH
F32 = jnp.float32
BF16 = jnp.bfloat16


def split(x):
    hi = x.astype(BF16)
    lo = (x - hi.astype(F32)).astype(BF16)
    return hi, lo


def product_kernel(
    n, m, a_hbm, basis, pat_v, pat_s, image_hbm, gram_out,
    a_vm, req_out, req_in, out_buf, land, stage, acc, part, gram_in, chunk,
    slot_s, index_s,
    a_sem, image_sem, req_send, req_recv, dat_send, dat_recv, rs_send, rs_recv, ag_send, ag_recv,
):
    me = lax.axis_index("rows")
    rows, slots = pat_s.shape
    cols = part.shape[1]
    share = chunk.shape[0]

    def offset(k):
        return n // 2 + ((k + 1) // 2) * (1 - 2 * (k % 2))

    def remote(src, dst, send, recv, target):
        return pltpu.make_async_remote_copy(
            src_ref=src, dst_ref=dst, send_sem=send, recv_sem=recv,
            device_id={"rows": target}, device_id_type=MESH,
        )

    barrier = pltpu.get_barrier_semaphore()

    @pl.loop(0, n - 1)
    def _(k):
        pl.semaphore_signal(
            barrier, inc=1, device_id={"rows": (me + k + 1) % n}, device_id_type=MESH
        )

    a_copy = pltpu.make_async_copy(a_hbm, a_vm, a_sem)
    a_copy.start()
    pattern = pat_v[...][None]
    owner_ids = lax.broadcasted_iota(jnp.int32, (n, rows, slots), 0)
    local = pattern - owner_ids * rows
    named = jnp.where((local >= 0) & (local < rows), local, 0)
    asked = jnp.max(jnp.max(named, axis=2, keepdims=True), axis=1, keepdims=True)
    req_out[...] = jnp.broadcast_to(asked, req_out.shape)
    pl.semaphore_wait(barrier, n - 1)

    @pl.loop(0, n - 1)
    def _(k):
        target = (me + n - offset(k)) % n
        remote(
            req_out.at[target], req_in.at[me], req_send.at[target], req_recv.at[me], target
        ).start()

    @pl.loop(0, n - 1)
    def _(k):
        target = (me + offset(k)) % n
        remote(
            req_out.at[target], req_in.at[target], req_send.at[target], req_recv.at[target], target
        ).wait_recv()
        wanted = req_in[target][0, 0]
        out_buf[target] = basis[wanted]
        remote(
            out_buf.at[target], land.at[me], dat_send.at[target], dat_recv.at[me], target
        ).start()

    for b in range(rows):
        stage[b] = basis[b]

    @pl.loop(0, rows)
    def _(r):
        keys = []
        places = []
        for s in range(slots):
            col = pat_s[r, s]
            owner = col // rows
            delta = (me - owner + n) % n - n // 2
            rank = jnp.where(delta > 0, 2 * delta, -2 * delta - 1)
            rank = jnp.where(delta == 0, 0, rank)
            rank = jnp.where(owner == me, -1, rank)
            keys.append(rank * slots + s)
            places.append(jnp.where(owner == me, col - owner * rows, rows + owner))
        position = []
        for s in range(slots):
            count = 0
            for t in range(slots):
                if t != s:
                    count = count + jnp.where(keys[t] < keys[s], 1, 0)
            position.append(count)
        for k in range(slots):
            slot = 0
            place = 0
            for s in range(slots):
                slot = jnp.where(position[s] == k, s, slot)
                place = jnp.where(position[s] == k, places[s], place)
            slot_s[r, k] = slot
            index_s[r, k] = place

    def arrive(k):
        source = (me + n - offset(k)) % n
        remote(
            out_buf.at[source], land.at[source], dat_send.at[source], dat_recv.at[source], source
        ).wait_recv()
        stage[rows + source] = land[source]

    @pl.loop(0, n - 1 - slots)
    def _(k):
        arrive(k)

    a_copy.wait()

    for k in range(slots):
        arrive(n - 1 - slots + k)

        @pl.loop(0, rows)
        def _(r):
            term = jnp.dot(
                a_vm[r, slot_s[r, k]], stage[index_s[r, k]], preferred_element_type=F32
            )
            if k == 0:
                acc[r] = term
            else:
                acc[r] += term

    image_copy = pltpu.make_async_copy(acc, image_hbm, image_sem)
    image_copy.start()

    total = jnp.zeros((cols, 2 * cols), F32)
    for r in range(rows):
        hi, lo = split(acc[r])
        total = total + lax.dot_general(
            hi, jnp.concatenate([hi, lo], axis=1), (((0,), (0,)), ((), ())),
            preferred_element_type=F32,
        )
    cross = total[:, cols:]
    part[...] = total[:, :cols] + cross + cross.T

    @pl.loop(0, m)
    def _(t):
        @pl.when(t != me)
        def _():
            remote(
                part.at[pl.ds(t * share, share)], gram_in.at[me], rs_send.at[t], rs_recv.at[me], t
            ).start()

    @pl.when(me < m)
    def _():
        gram_in[me] = part[pl.ds(pl.multiple_of(me * share, share), share), :]

        @pl.loop(0, n - 1)
        def _(k):
            source = (me + k + 1) % n
            remote(
                part.at[pl.ds(0, share)], gram_in.at[source], rs_send.at[0], rs_recv.at[source], source
            ).wait_recv()

        chunk[...] = jnp.sum(gram_in[...], axis=0)

        @pl.loop(0, n - 1)
        def _(k):
            target = (me + k + 1) % n
            remote(
                chunk, gram_out.at[pl.ds(me * share, share)], ag_send.at[target], ag_recv.at[me], target
            ).start()

        gram_out[pl.ds(pl.multiple_of(me * share, share), share), :] = chunk[...]

    @pl.loop(0, m)
    def _(t):
        @pl.when(t != me)
        def _():
            remote(
                chunk, gram_out.at[pl.ds(t * share, share)], ag_send.at[t], ag_recv.at[t], t
            ).wait_recv()
            remote(
                part.at[pl.ds(t * share, share)], gram_in.at[me], rs_send.at[t], rs_recv.at[me], t
            ).wait_send()

    @pl.when(me < m)
    def _():
        @pl.loop(0, n - 1)
        def _(k):
            target = (me + k + 1) % n
            remote(
                chunk, gram_out.at[pl.ds(me * share, share)], ag_send.at[target], ag_recv.at[me], target
            ).wait_send()

    @pl.loop(0, n - 1)
    def _(k):
        target = (me + k + 1) % n
        remote(
            req_out.at[target], req_in.at[me], req_send.at[target], req_recv.at[me], target
        ).wait_send()
        remote(
            out_buf.at[target], land.at[me], dat_send.at[target], dat_recv.at[me], target
        ).wait_send()

    image_copy.wait()


def product_and_gram(a_blocks, own_blocks, pattern):
    n = lax.axis_size("rows")
    rows, slots, size, unused = a_blocks.shape
    cols = own_blocks.shape[2]
    share = 8
    m = cols // share
    assert n >= m and n > slots
    vmem = pl.BlockSpec(memory_space=pltpu.VMEM)
    dma = pltpu.SemaphoreType.DMA
    return pl.pallas_call(
        functools.partial(product_kernel, n, m),
        out_shape=(
            jax.ShapeDtypeStruct((rows, size, cols), F32),
            jax.ShapeDtypeStruct((cols, cols), F32),
        ),
        in_specs=[
            pl.BlockSpec(memory_space=pl.ANY), vmem, vmem, pl.BlockSpec(memory_space=pltpu.SMEM),
        ],
        out_specs=(pl.BlockSpec(memory_space=pl.ANY), vmem),
        scratch_shapes=[
            pltpu.VMEM(a_blocks.shape, BF16),
            pltpu.VMEM((n, 1, 128), jnp.int32),
            pltpu.VMEM((n, 1, 128), jnp.int32),
            pltpu.VMEM((n, size, cols), BF16),
            pltpu.VMEM((n, size, cols), BF16),
            pltpu.VMEM((rows + n, size, cols), BF16),
            pltpu.VMEM((rows, size, cols), F32),
            pltpu.VMEM((cols, cols), F32),
            pltpu.VMEM((n, share, cols), F32),
            pltpu.VMEM((share, cols), F32),
            pltpu.SMEM((rows, slots), jnp.int32),
            pltpu.SMEM((rows, slots), jnp.int32),
            dma, dma,
            dma((n,)), dma((n,)), dma((n,)), dma((n,)),
            dma((n,)), dma((n,)), dma((n,)), dma((n,)),
        ],
        compiler_params=pltpu.CompilerParams(
            collective_id=0, has_side_effects=True, vmem_limit_bytes=52 * 1024 * 1024
        ),
        name="product_and_gram",
    )(a_blocks, own_blocks, pattern, pattern)


def shards(a_blocks, basis_in, pattern):
    n = lax.axis_size("rows")
    rows, slots, size, unused = a_blocks.shape
    cols = basis_in.shape[1]
    image, gram = product_and_gram(a_blocks, basis_in.reshape(rows, size, cols), pattern)
    image = image.reshape(rows * size, cols)
    factor = jnp.linalg.cholesky(gram / (n * rows * size)).T
    basis_out = jax.scipy.linalg.solve_triangular(factor.T, image.T, lower=True).T
    return (basis_out, factor)


def solution(mesh):
    placed = (
        P(("groups", "rows"), None, None, None),
        P(("groups", "rows"), None),
        P(("groups", "rows"), None),
    )
    return jax.shard_map(
        shards,
        mesh=mesh,
        in_specs=placed,
        out_specs=(P(("groups", "rows"), None), P("groups", None)),
        check_vma=False,
    )
```

```python
import functools
import jax
import jax.numpy as jnp
from jax import lax
from jax.experimental import pallas as pl
from jax.experimental.pallas import tpu as pltpu
from jax.sharding import PartitionSpec as P

MESH = pl.DeviceIdType.MESH
F32 = jnp.float32
BF16 = jnp.bfloat16
STEP = 16


def split(x):
    hi = x.astype(BF16)
    lo = (x - hi.astype(F32)).astype(BF16)
    return hi, lo


def product_kernel(
    n, m, a_hbm, basis, pat_v, pat_s, image_hbm, gram_out,
    a_vm, req_out, req_in, out_buf, land, stage, acc, part, gram_in, chunk,
    slot_s, index_s,
    a_sem, image_sem, req_send, req_recv, dat_send, dat_recv, rs_send, rs_recv, ag_send, ag_recv,
):
    me = lax.axis_index("rows")
    rows, slots = pat_s.shape
    cols = part.shape[1]
    share = chunk.shape[0]

    def partner(k):
        d = k + 1
        other = me + d
        bit = 1
        while bit < n:
            other = other - 2 * bit * ((me // bit) % 2) * ((d // bit) % 2)
            bit *= 2
        return other

    def remote(src, dst, send, recv, target):
        return pltpu.make_async_remote_copy(
            src_ref=src, dst_ref=dst, send_sem=send, recv_sem=recv,
            device_id={"rows": target}, device_id_type=MESH,
        )

    barrier = pltpu.get_barrier_semaphore()

    @pl.loop(0, n - 1)
    def _(k):
        pl.semaphore_signal(
            barrier, inc=1, device_id={"rows": (me + k + 1) % n}, device_id_type=MESH
        )

    a_copy = pltpu.make_async_copy(a_hbm, a_vm, a_sem)
    a_copy.start()
    pattern = pat_v[...][None]
    owner_ids = lax.broadcasted_iota(jnp.int32, (n, rows, slots), 0)
    local = pattern - owner_ids * rows
    named = jnp.where((local >= 0) & (local < rows), local, 0)
    asked = jnp.max(jnp.max(named, axis=2, keepdims=True), axis=1, keepdims=True)
    req_out[...] = jnp.broadcast_to(asked, req_out.shape)
    pl.semaphore_wait(barrier, n - 1)

    @pl.loop(0, n - 1)
    def _(k):
        target = partner(k)
        remote(
            req_out.at[target], req_in.at[me], req_send.at[target], req_recv.at[me], target
        ).start()

    @pl.loop(0, n - 1)
    def _(k):
        target = partner(k)
        remote(
            req_out.at[target], req_in.at[target], req_send.at[target], req_recv.at[target], target
        ).wait_recv()
        wanted = req_in[target][0, 0]
        out_buf[target] = basis[wanted]
        remote(
            out_buf.at[target], land.at[me], dat_send.at[target], dat_recv.at[me], target
        ).start()

    for b in range(rows):
        stage[b] = basis[b]

    @pl.loop(0, rows)
    def _(r):
        keys = []
        places = []
        for s in range(slots):
            col = pat_s[r, s]
            owner = col // rows
            rank = jnp.bitwise_xor(owner, me)
            keys.append(rank * slots + s)
            places.append(jnp.where(owner == me, col - owner * rows, rows + owner))
        position = []
        for s in range(slots):
            count = 0
            for t in range(slots):
                if t != s:
                    count = count + jnp.where(keys[t] < keys[s], 1, 0)
            position.append(count)
        for k in range(slots):
            slot = 0
            place = 0
            for s in range(slots):
                slot = jnp.where(position[s] == k, s, slot)
                place = jnp.where(position[s] == k, places[s], place)
            slot_s[r, k] = slot
            index_s[r, k] = place

    def arrive(k):
        source = partner(k)
        remote(
            out_buf.at[source], land.at[source], dat_send.at[source], dat_recv.at[source], source
        ).wait_recv()
        stage[rows + source] = land[source]

    @pl.loop(0, n - 1 - slots)
    def _(k):
        arrive(k)

    a_copy.wait()

    for k in range(slots):
        arrive(n - 1 - slots + k)

        @pl.loop(0, rows)
        def _(r):
            term = jnp.dot(
                a_vm[r, slot_s[r, k]], stage[index_s[r, k]], preferred_element_type=F32
            )
            if k == 0:
                acc[r] = term
            else:
                acc[r] += term

    image_copy = pltpu.make_async_copy(acc, image_hbm, image_sem)
    image_copy.start()

    total = jnp.zeros((cols, 2 * cols), F32)
    for r in range(rows):
        hi, lo = split(acc[r])
        total = total + lax.dot_general(
            hi, jnp.concatenate([hi, lo], axis=1), (((0,), (0,)), ((), ())),
            preferred_element_type=F32,
        )
    cross = total[:, cols:]
    part[...] = total[:, :cols] + cross + cross.T

    @pl.loop(0, m)
    def _(t):
        @pl.when(t != me)
        def _():
            remote(
                part.at[pl.ds(t * share, share)], gram_in.at[me], rs_send.at[t], rs_recv.at[me], t
            ).start()

    @pl.when(me < m)
    def _():
        gram_in[me] = part[pl.ds(pl.multiple_of(me * share, share), share), :]

        @pl.loop(0, n - 1)
        def _(k):
            source = (me + k + 1) % n
            remote(
                part.at[pl.ds(0, share)], gram_in.at[source], rs_send.at[0], rs_recv.at[source], source
            ).wait_recv()

        chunk[...] = jnp.sum(gram_in[...], axis=0)

        @pl.loop(0, n - 1)
        def _(k):
            target = (me + k + 1) % n
            remote(
                chunk, gram_out.at[pl.ds(me * share, share)], ag_send.at[target], ag_recv.at[me], target
            ).start()

        gram_out[pl.ds(pl.multiple_of(me * share, share), share), :] = chunk[...]

    @pl.loop(0, m)
    def _(t):
        @pl.when(t != me)
        def _():
            remote(
                chunk, gram_out.at[pl.ds(t * share, share)], ag_send.at[t], ag_recv.at[t], t
            ).wait_recv()
            remote(
                part.at[pl.ds(t * share, share)], gram_in.at[me], rs_send.at[t], rs_recv.at[me], t
            ).wait_send()

    @pl.when(me < m)
    def _():
        @pl.loop(0, n - 1)
        def _(k):
            target = (me + k + 1) % n
            remote(
                chunk, gram_out.at[pl.ds(me * share, share)], ag_send.at[target], ag_recv.at[me], target
            ).wait_send()

    @pl.loop(0, n - 1)
    def _(k):
        target = (me + k + 1) % n
        remote(
            req_out.at[target], req_in.at[me], req_send.at[target], req_recv.at[me], target
        ).wait_send()
        remote(
            out_buf.at[target], land.at[me], dat_send.at[target], dat_recv.at[me], target
        ).wait_send()

    image_copy.wait()


def product_and_gram(a_blocks, own_blocks, pattern):
    n = lax.axis_size("rows")
    rows, slots, size, unused = a_blocks.shape
    cols = own_blocks.shape[2]
    share = 8
    m = cols // share
    assert n >= m and n > slots and n & (n - 1) == 0
    vmem = pl.BlockSpec(memory_space=pltpu.VMEM)
    dma = pltpu.SemaphoreType.DMA
    return pl.pallas_call(
        functools.partial(product_kernel, n, m),
        out_shape=(
            jax.ShapeDtypeStruct((rows, size, cols), F32),
            jax.ShapeDtypeStruct((cols, cols), F32),
        ),
        in_specs=[
            pl.BlockSpec(memory_space=pl.ANY), vmem, vmem, pl.BlockSpec(memory_space=pltpu.SMEM),
        ],
        out_specs=(pl.BlockSpec(memory_space=pl.ANY), vmem),
        scratch_shapes=[
            pltpu.VMEM(a_blocks.shape, BF16),
            pltpu.VMEM((n, 1, 128), jnp.int32),
            pltpu.VMEM((n, 1, 128), jnp.int32),
            pltpu.VMEM((n, size, cols), BF16),
            pltpu.VMEM((n, size, cols), BF16),
            pltpu.VMEM((rows + n, size, cols), BF16),
            pltpu.VMEM((rows, size, cols), F32),
            pltpu.VMEM((cols, cols), F32),
            pltpu.VMEM((n, share, cols), F32),
            pltpu.VMEM((share, cols), F32),
            pltpu.SMEM((rows, slots), jnp.int32),
            pltpu.SMEM((rows, slots), jnp.int32),
            dma, dma,
            dma((n,)), dma((n,)), dma((n,)), dma((n,)),
            dma((n,)), dma((n,)), dma((n,)), dma((n,)),
        ],
        compiler_params=pltpu.CompilerParams(
            collective_id=0, has_side_effects=True, vmem_limit_bytes=52 * 1024 * 1024
        ),
        name="product_and_gram",
    )(a_blocks, own_blocks, pattern, pattern)


def lanes(x, width):
    return jnp.broadcast_to(x, (x.shape[0], width))


def sublanes(x, i):
    return jnp.broadcast_to(x[i:i + 1], x.shape)


def three(x):
    high = x.astype(BF16).astype(F32)
    rest = x - high
    middle = rest.astype(BF16).astype(F32)
    return high, middle, rest - middle


def factor_kernel(scale, step, gram, image_hbm, basis_hbm, factor, image, result, in_sem, out_sem):
    cols = gram.shape[0]
    chunks, size, unused = image.shape
    image_copy = pltpu.make_async_copy(image_hbm, image, in_sem)
    image_copy.start()
    down = lax.broadcasted_iota(jnp.int32, (cols, cols), 0)
    across = lax.broadcasted_iota(jnp.int32, (cols, cols), 1)
    rest = jnp.concatenate([gram[...] * scale, jnp.where(down == across, 1.0, 0.0)], axis=1)
    halves = step // 8
    sub = lax.broadcasted_iota(jnp.int32, (8, cols), 0)
    uppers = []
    lowers = []
    for start in range(0, cols, step):
        panel = [rest[8 * h:8 * h + 8] for h in range(halves)]
        column = [
            [lanes(panel[h][:, start + l:start + l + 1], cols) for h in range(halves)]
            for l in range(step)
        ]
        left = [p[:, :cols] for p in panel]
        right = [p[:, cols:] for p in panel]
        pivots = [jnp.ones((8, cols), F32) for h in range(halves)]
        for k in range(step):
            h0, i0 = divmod(k, 8)
            pivot = sublanes(column[k][h0], i0)
            pivots[h0] = jnp.where(sub == i0, pivot, pivots[h0])
            inverse = 1.0 / pivot
            below = [
                jnp.where(sub > i0, column[k][h], 0.0) if h == h0 else column[k][h]
                for h in range(h0, halves)
            ]
            for l in range(k + 1, step):
                weight = sublanes(column[l][h0], i0) * inverse
                for h in range(h0, halves):
                    column[l][h] = column[l][h] - below[h - h0] * weight
            top_left = sublanes(left[h0], i0) * inverse
            top_right = sublanes(right[h0], i0) * inverse
            for h in range(h0, halves):
                left[h] = left[h] - below[h - h0] * top_left
                right[h] = right[h] - below[h - h0] * top_right
        roots = [lax.rsqrt(p) for p in pivots]
        new_left = jnp.concatenate([l * r for l, r in zip(left, roots)], axis=0)
        new_right = jnp.concatenate([l * r for l, r in zip(right, roots)], axis=0)
        uppers.append(new_left)
        lowers.append(new_right)
        if start + step < cols:
            a1, a2, a3 = three(new_left)
            b1, b2, b3 = three(new_right)
            lhs = jnp.concatenate([a1, a1, a2, a2, a1, a3], axis=0).astype(BF16)
            rhs = jnp.concatenate(
                [
                    jnp.concatenate([a1, a2, a1, a2, a3, a1], axis=0),
                    jnp.concatenate([b1, b2, b1, b2, b3, b1], axis=0),
                ],
                axis=1,
            ).astype(BF16)
            change = lax.dot_general(
                lhs, rhs, (((0,), (0,)), ((), ())), preferred_element_type=F32
            )
            rest = rest[step:] - change[start + step:]
    upper = jnp.concatenate(uppers, axis=0)
    lower = jnp.concatenate(lowers, axis=0)
    factor[...] = jnp.where(across >= down, upper, 0.0)
    high, low = split(lower)
    both = jnp.concatenate([high, high], axis=1)
    image_copy.wait()
    turned = (((1,), (1,)), ((), ()))
    for c in range(chunks):
        x_high, x_low = split(image[c])
        result[c] = lax.dot_general(
            jnp.concatenate([x_high, x_low], axis=1), both, turned, preferred_element_type=F32
        ) + lax.dot_general(x_high, low, turned, preferred_element_type=F32)
        pltpu.make_async_copy(result.at[c], basis_hbm.at[c], out_sem.at[c]).start()
    for c in range(chunks):
        pltpu.make_async_copy(result.at[c], basis_hbm.at[c], out_sem.at[c]).wait()


def factor_and_basis(gram, image, nodes):
    vmem = pl.BlockSpec(memory_space=pltpu.VMEM)
    dma = pltpu.SemaphoreType.DMA
    return pl.pallas_call(
        functools.partial(factor_kernel, 1.0 / nodes, STEP),
        out_shape=(
            jax.ShapeDtypeStruct(image.shape, F32),
            jax.ShapeDtypeStruct(gram.shape, F32),
        ),
        in_specs=[vmem, pl.BlockSpec(memory_space=pl.ANY)],
        out_specs=(pl.BlockSpec(memory_space=pl.ANY), vmem),
        scratch_shapes=[
            pltpu.VMEM(image.shape, F32), pltpu.VMEM(image.shape, F32), dma, dma((image.shape[0],)),
        ],
        compiler_params=pltpu.CompilerParams(vmem_limit_bytes=32 * 1024 * 1024),
        name="factor_and_basis",
    )(gram, image)


def shards(a_blocks, basis_in, pattern):
    n = lax.axis_size("rows")
    rows, slots, size, unused = a_blocks.shape
    cols = basis_in.shape[1]
    image, gram = product_and_gram(a_blocks, basis_in.reshape(rows, size, cols), pattern)
    basis_out, factor = factor_and_basis(gram, image, n * rows * size)
    return (basis_out.reshape(rows * size, cols), factor)


def solution(mesh):
    placed = (
        P(("groups", "rows"), None, None, None),
        P(("groups", "rows"), None),
        P(("groups", "rows"), None),
    )
    return jax.shard_map(
        shards,
        mesh=mesh,
        in_specs=placed,
        out_specs=(P(("groups", "rows"), None), P("groups", None)),
        check_vma=False,
    )
```

```python
import functools
import jax
import jax.numpy as jnp
from jax import lax
from jax.experimental import pallas as pl
from jax.experimental.pallas import tpu as pltpu
from jax.sharding import PartitionSpec as P

MESH = pl.DeviceIdType.MESH
F32 = jnp.float32
BF16 = jnp.bfloat16
STEP = 16


def split(x):
    hi = x.astype(BF16)
    lo = (x - hi.astype(F32)).astype(BF16)
    return hi, lo


def product_kernel(
    n, m, a_hbm, basis_hbm, pat_hbm, image_hbm, gram_out,
    pat_v, pat_s, a_vm, req_out, req_in, out_buf, land, stage, acc, part, gram_in, chunk,
    slot_s, index_s,
    a_sem, basis_sem, pat_v_sem, pat_s_sem, image_sem, req_send, req_recv, dat_send, dat_recv, rs_send, rs_recv, ag_send, ag_recv,
):
    me = lax.axis_index("rows")
    rows, slots = pat_s.shape
    cols = part.shape[1]
    share = chunk.shape[0]

    def partner(k):
        d = k + 1
        other = me + d
        bit = 1
        while bit < n:
            other = other - 2 * bit * ((me // bit) % 2) * ((d // bit) % 2)
            bit *= 2
        return other

    def remote(src, dst, send, recv, target):
        return pltpu.make_async_remote_copy(
            src_ref=src, dst_ref=dst, send_sem=send, recv_sem=recv,
            device_id={"rows": target}, device_id_type=MESH,
        )

    unroll = n <= 16
    pat_v_copy = pltpu.make_async_copy(pat_hbm, pat_v, pat_v_sem)
    pat_v_copy.start()
    pat_s_copy = pltpu.make_async_copy(pat_hbm, pat_s, pat_s_sem)
    pat_s_copy.start()
    basis_copy = pltpu.make_async_copy(basis_hbm, stage.at[pl.ds(0, rows)], basis_sem)
    basis_copy.start()
    barrier = pltpu.get_barrier_semaphore()

    @pl.loop(0, n - 1, unroll=unroll)
    def _(k):
        pl.semaphore_signal(
            barrier, inc=1, device_id={"rows": (me + k + 1) % n}, device_id_type=MESH
        )

    a_copy = pltpu.make_async_copy(a_hbm, a_vm, a_sem)
    a_copy.start()
    pat_v_copy.wait()
    pattern = pat_v[...][None]
    owner_ids = lax.broadcasted_iota(jnp.int32, (n, rows, slots), 0)
    local = pattern - owner_ids * rows
    named = jnp.where((local >= 0) & (local < rows), local, 0)
    asked = jnp.max(jnp.max(named, axis=2, keepdims=True), axis=1, keepdims=True)
    req_out[...] = jnp.broadcast_to(asked, req_out.shape)
    basis_copy.wait()
    pat_s_copy.wait()
    pl.semaphore_wait(barrier, n - 1)

    @pl.loop(0, n - 1, unroll=unroll)
    def _(k):
        target = partner(k)
        remote(
            req_out.at[target], req_in.at[me], req_send.at[target], req_recv.at[me], target
        ).start()

    @pl.loop(0, n - 1, unroll=unroll)
    def _(k):
        target = partner(k)
        remote(
            req_out.at[target], req_in.at[target], req_send.at[target], req_recv.at[target], target
        ).wait_recv()
        wanted = req_in[target][0, 0]
        out_buf[target] = stage[wanted]
        remote(
            out_buf.at[target], land.at[me], dat_send.at[target], dat_recv.at[me], target
        ).start()

    @pl.loop(0, rows)
    def _(r):
        keys = []
        places = []
        for s in range(slots):
            col = pat_s[r, s]
            owner = col // rows
            rank = jnp.bitwise_xor(owner, me)
            keys.append(rank * slots + s)
            places.append(jnp.where(owner == me, col - owner * rows, rows + owner))
        position = []
        for s in range(slots):
            count = 0
            for t in range(slots):
                if t != s:
                    count = count + jnp.where(keys[t] < keys[s], 1, 0)
            position.append(count)
        for k in range(slots):
            slot = 0
            place = 0
            for s in range(slots):
                slot = jnp.where(position[s] == k, s, slot)
                place = jnp.where(position[s] == k, places[s], place)
            slot_s[r, k] = slot
            index_s[r, k] = place

    def arrive(k):
        source = partner(k)
        remote(
            out_buf.at[source], land.at[source], dat_send.at[source], dat_recv.at[source], source
        ).wait_recv()
        stage[rows + source] = land[source]

    @pl.loop(0, n - 1 - slots)
    def _(k):
        arrive(k)

    a_copy.wait()

    for k in range(slots):
        arrive(n - 1 - slots + k)

        for r in range(rows):
            term = jnp.dot(
                a_vm[r, slot_s[r, k]], stage[index_s[r, k]], preferred_element_type=F32
            )
            if k > 0:
                term = term + acc[r]
            acc[r] = term
            if k == slots - 1:
                high, low = split(term)
                square = lax.dot_general(
                    high, jnp.concatenate([high, low], axis=1), (((0,), (0,)), ((), ())),
                    preferred_element_type=F32,
                )
                total = square if r == 0 else total + square

    image_copy = pltpu.make_async_copy(acc, image_hbm, image_sem)
    image_copy.start()
    cross = total[:, cols:]
    part[...] = total[:, :cols] + cross + cross.T

    @pl.loop(0, m, unroll=unroll)
    def _(t):
        @pl.when(t != me)
        def _():
            remote(
                part.at[pl.ds(t * share, share)], gram_in.at[me], rs_send.at[t], rs_recv.at[me], t
            ).start()

    @pl.when(me < m)
    def _():
        gram_in[me] = part[pl.ds(pl.multiple_of(me * share, share), share), :]

        @pl.loop(0, n - 1, unroll=unroll)
        def _(k):
            source = (me + k + 1) % n
            remote(
                part.at[pl.ds(0, share)], gram_in.at[source], rs_send.at[0], rs_recv.at[source], source
            ).wait_recv()

        chunk[...] = jnp.sum(gram_in[...], axis=0)

        @pl.loop(0, n - 1, unroll=unroll)
        def _(k):
            target = (me + k + 1) % n
            remote(
                chunk, gram_out.at[pl.ds(me * share, share)], ag_send.at[target], ag_recv.at[me], target
            ).start()

        gram_out[pl.ds(pl.multiple_of(me * share, share), share), :] = chunk[...]

    @pl.loop(0, m, unroll=unroll)
    def _(t):
        @pl.when(t != me)
        def _():
            remote(
                chunk, gram_out.at[pl.ds(t * share, share)], ag_send.at[t], ag_recv.at[t], t
            ).wait_recv()
            remote(
                part.at[pl.ds(t * share, share)], gram_in.at[me], rs_send.at[t], rs_recv.at[me], t
            ).wait_send()

    @pl.when(me < m)
    def _():
        @pl.loop(0, n - 1, unroll=unroll)
        def _(k):
            target = (me + k + 1) % n
            remote(
                chunk, gram_out.at[pl.ds(me * share, share)], ag_send.at[target], ag_recv.at[me], target
            ).wait_send()

    @pl.loop(0, n - 1, unroll=unroll)
    def _(k):
        target = (me + k + 1) % n
        remote(
            req_out.at[target], req_in.at[me], req_send.at[target], req_recv.at[me], target
        ).wait_send()
        remote(
            out_buf.at[target], land.at[me], dat_send.at[target], dat_recv.at[me], target
        ).wait_send()

    image_copy.wait()


def product_and_gram(a_blocks, own_blocks, pattern):
    n = lax.axis_size("rows")
    rows, slots, size, unused = a_blocks.shape
    cols = own_blocks.shape[2]
    share = 8
    m = cols // share
    assert n >= m and n > slots and n & (n - 1) == 0
    vmem = pl.BlockSpec(memory_space=pltpu.VMEM)
    dma = pltpu.SemaphoreType.DMA
    return pl.pallas_call(
        functools.partial(product_kernel, n, m),
        out_shape=(
            jax.ShapeDtypeStruct((rows, size, cols), F32),
            jax.ShapeDtypeStruct((cols, cols), F32),
        ),
        in_specs=[
            pl.BlockSpec(memory_space=pltpu.HBM),
            pl.BlockSpec(memory_space=pltpu.HBM),
            pl.BlockSpec(memory_space=pltpu.HBM),
        ],
        out_specs=(pl.BlockSpec(memory_space=pl.ANY), vmem),
        scratch_shapes=[
            pltpu.VMEM((rows, slots), jnp.int32),
            pltpu.SMEM((rows, slots), jnp.int32),
            pltpu.VMEM(a_blocks.shape, BF16),
            pltpu.VMEM((n, 1, 128), jnp.int32),
            pltpu.VMEM((n, 1, 128), jnp.int32),
            pltpu.VMEM((n, size, cols), BF16),
            pltpu.VMEM((n, size, cols), BF16),
            pltpu.VMEM((rows + n, size, cols), BF16),
            pltpu.VMEM((rows, size, cols), F32),
            pltpu.VMEM((cols, cols), F32),
            pltpu.VMEM((n, share, cols), F32),
            pltpu.VMEM((share, cols), F32),
            pltpu.SMEM((rows, slots), jnp.int32),
            pltpu.SMEM((rows, slots), jnp.int32),
            dma, dma, dma, dma, dma,
            dma((n,)), dma((n,)), dma((n,)), dma((n,)),
            dma((n,)), dma((n,)), dma((n,)), dma((n,)),
        ],
        compiler_params=pltpu.CompilerParams(
            collective_id=0, has_side_effects=True, vmem_limit_bytes=52 * 1024 * 1024
        ),
        name="product_and_gram",
    )(a_blocks, own_blocks, pattern)


def lanes(x, width):
    return jnp.broadcast_to(x, (x.shape[0], width))


def sublanes(x, i):
    return jnp.broadcast_to(x[i:i + 1], x.shape)


def three(x):
    high = x.astype(BF16).astype(F32)
    rest = x - high
    middle = rest.astype(BF16).astype(F32)
    return high, middle, rest - middle


def factor_kernel(scale, step, gram, image_hbm, basis_hbm, factor, image, result, in_sem, out_sem):
    cols = gram.shape[0]
    chunks, size, unused = image.shape
    image_copy = pltpu.make_async_copy(image_hbm, image, in_sem)
    image_copy.start()
    down = lax.broadcasted_iota(jnp.int32, (cols, cols), 0)
    across = lax.broadcasted_iota(jnp.int32, (cols, cols), 1)
    rest = jnp.concatenate([gram[...] * scale, jnp.where(down == across, 1.0, 0.0)], axis=1)
    halves = step // 8
    sub = lax.broadcasted_iota(jnp.int32, (8, cols), 0)
    uppers = []
    lowers = []
    for start in range(0, cols, step):
        panel = [rest[8 * h:8 * h + 8] for h in range(halves)]
        column = [
            [lanes(panel[h][:, start + l:start + l + 1], cols) for h in range(halves)]
            for l in range(step)
        ]
        left = [p[:, :cols] for p in panel]
        right = [p[:, cols:] for p in panel]
        pivots = [jnp.ones((8, cols), F32) for h in range(halves)]
        for k in range(step):
            h0, i0 = divmod(k, 8)
            pivot = sublanes(column[k][h0], i0)
            pivots[h0] = jnp.where(sub == i0, pivot, pivots[h0])
            inverse = 1.0 / pivot
            below = [
                jnp.where(sub > i0, column[k][h], 0.0) if h == h0 else column[k][h]
                for h in range(h0, halves)
            ]
            for l in range(k + 1, step):
                weight = sublanes(column[l][h0], i0) * inverse
                for h in range(h0, halves):
                    column[l][h] = column[l][h] - below[h - h0] * weight
            top_left = sublanes(left[h0], i0) * inverse
            top_right = sublanes(right[h0], i0) * inverse
            for h in range(h0, halves):
                left[h] = left[h] - below[h - h0] * top_left
                right[h] = right[h] - below[h - h0] * top_right
        roots = [lax.rsqrt(p) for p in pivots]
        new_left = jnp.concatenate([l * r for l, r in zip(left, roots)], axis=0)
        new_right = jnp.concatenate([l * r for l, r in zip(right, roots)], axis=0)
        uppers.append(new_left)
        lowers.append(new_right)
        if start + step < cols:
            a1, a2, a3 = three(new_left)
            b1, b2, b3 = three(new_right)
            lhs = jnp.concatenate([a1, a1, a2, a2, a1, a3], axis=0).astype(BF16)
            rhs = jnp.concatenate(
                [
                    jnp.concatenate([a1, a2, a1, a2, a3, a1], axis=0),
                    jnp.concatenate([b1, b2, b1, b2, b3, b1], axis=0),
                ],
                axis=1,
            ).astype(BF16)
            change = lax.dot_general(
                lhs, rhs, (((0,), (0,)), ((), ())), preferred_element_type=F32
            )
            rest = rest[step:] - change[start + step:]
    upper = jnp.concatenate(uppers, axis=0)
    lower = jnp.concatenate(lowers, axis=0)
    factor[...] = jnp.where(across >= down, upper, 0.0)
    high, low = split(lower)
    both = jnp.concatenate([high, high], axis=1)
    image_copy.wait()
    turned = (((1,), (1,)), ((), ()))
    for c in range(chunks):
        x_high, x_low = split(image[c])
        result[c] = lax.dot_general(
            jnp.concatenate([x_high, x_low], axis=1), both, turned, preferred_element_type=F32
        ) + lax.dot_general(x_high, low, turned, preferred_element_type=F32)
        pltpu.make_async_copy(result.at[c], basis_hbm.at[c], out_sem.at[c]).start()
    for c in range(chunks):
        pltpu.make_async_copy(result.at[c], basis_hbm.at[c], out_sem.at[c]).wait()


def factor_and_basis(gram, image, nodes):
    vmem = pl.BlockSpec(memory_space=pltpu.VMEM)
    dma = pltpu.SemaphoreType.DMA
    return pl.pallas_call(
        functools.partial(factor_kernel, 1.0 / nodes, STEP),
        out_shape=(
            jax.ShapeDtypeStruct(image.shape, F32),
            jax.ShapeDtypeStruct(gram.shape, F32),
        ),
        in_specs=[vmem, pl.BlockSpec(memory_space=pl.ANY)],
        out_specs=(pl.BlockSpec(memory_space=pl.ANY), vmem),
        scratch_shapes=[
            pltpu.VMEM(image.shape, F32), pltpu.VMEM(image.shape, F32), dma, dma((image.shape[0],)),
        ],
        compiler_params=pltpu.CompilerParams(vmem_limit_bytes=32 * 1024 * 1024),
        name="factor_and_basis",
    )(gram, image)


def shards(a_blocks, basis_in, pattern):
    n = lax.axis_size("rows")
    rows, slots, size, unused = a_blocks.shape
    cols = basis_in.shape[1]
    image, gram = product_and_gram(a_blocks, basis_in.reshape(rows, size, cols), pattern)
    basis_out, factor = factor_and_basis(gram, image, n * rows * size)
    return (basis_out.reshape(rows * size, cols), factor)


def solution(mesh):
    placed = (
        P(("groups", "rows"), None, None, None),
        P(("groups", "rows"), None),
        P(("groups", "rows"), None),
    )
    return jax.shard_map(
        shards,
        mesh=mesh,
        in_specs=placed,
        out_specs=(P(("groups", "rows"), None), P("groups", None)),
        check_vma=False,
    )
```

```python
import functools
import jax
import jax.numpy as jnp
from jax import lax
from jax.experimental import pallas as pl
from jax.experimental.pallas import tpu as pltpu
from jax.sharding import PartitionSpec as P

MESH = pl.DeviceIdType.MESH
F32 = jnp.float32
BF16 = jnp.bfloat16
STEP = 16


def split(x):
    hi = x.astype(BF16)
    lo = (x - hi.astype(F32)).astype(BF16)
    return hi, lo


def product_kernel(
    n, m, a_hbm, basis_hbm, pat_hbm, image_hbm, gram_out,
    pat_v, pat_s, a_vm, req_out, req_in, out_buf, land, stage, acc, part, gram_in, chunk,
    slot_s, index_s,
    a_sem, basis_sem, pat_v_sem, pat_s_sem, image_sem, req_send, req_recv, dat_send, dat_recv, rs_send, rs_recv, ag_send, ag_recv,
):
    me = lax.axis_index("rows")
    rows, slots = pat_s.shape
    cols = part.shape[1]
    share = chunk.shape[0]

    def partner(k):
        d = k + 1
        other = me + d
        bit = 1
        while bit < n:
            other = other - 2 * bit * ((me // bit) % 2) * ((d // bit) % 2)
            bit *= 2
        return other

    def remote(src, dst, send, recv, target):
        return pltpu.make_async_remote_copy(
            src_ref=src, dst_ref=dst, send_sem=send, recv_sem=recv,
            device_id={"rows": target}, device_id_type=MESH,
        )

    unroll = n <= 16
    pat_v_copy = pltpu.make_async_copy(pat_hbm, pat_v, pat_v_sem)
    pat_v_copy.start()
    pat_s_copy = pltpu.make_async_copy(pat_hbm, pat_s, pat_s_sem)
    pat_s_copy.start()
    basis_copy = pltpu.make_async_copy(basis_hbm, stage.at[pl.ds(0, rows)], basis_sem)
    basis_copy.start()
    barrier = pltpu.get_barrier_semaphore()

    @pl.loop(0, n - 1, unroll=unroll)
    def _(k):
        pl.semaphore_signal(
            barrier, inc=1, device_id={"rows": (me + k + 1) % n}, device_id_type=MESH
        )

    a_copy = pltpu.make_async_copy(a_hbm, a_vm, a_sem)
    a_copy.start()
    pat_v_copy.wait()
    pattern = pat_v[...][None]
    owner_ids = lax.broadcasted_iota(jnp.int32, (n, rows, slots), 0)
    local = pattern - owner_ids * rows
    named = jnp.where((local >= 0) & (local < rows), local, 0)
    asked = jnp.max(jnp.max(named, axis=2, keepdims=True), axis=1, keepdims=True)
    req_out[...] = jnp.broadcast_to(asked, req_out.shape)
    basis_copy.wait()
    pat_s_copy.wait()
    pl.semaphore_wait(barrier, n - 1)

    @pl.loop(0, n - 1, unroll=unroll)
    def _(k):
        target = partner(k)
        remote(
            req_out.at[target], req_in.at[me], req_send.at[target], req_recv.at[me], target
        ).start()

    @pl.loop(0, n - 1, unroll=unroll)
    def _(k):
        target = partner(k)
        remote(
            req_out.at[target], req_in.at[target], req_send.at[target], req_recv.at[target], target
        ).wait_recv()
        wanted = req_in[target][0, 0]
        out_buf[target] = stage[wanted]
        remote(
            out_buf.at[target], land.at[me], dat_send.at[target], dat_recv.at[me], target
        ).start()

    @pl.loop(0, rows)
    def _(r):
        keys = []
        places = []
        for s in range(slots):
            col = pat_s[r, s]
            owner = col // rows
            rank = jnp.bitwise_xor(owner, me)
            keys.append(rank * slots + s)
            places.append(jnp.where(owner == me, col - owner * rows, rows + owner))
        position = []
        for s in range(slots):
            count = 0
            for t in range(slots):
                if t != s:
                    count = count + jnp.where(keys[t] < keys[s], 1, 0)
            position.append(count)
        for k in range(slots):
            slot = 0
            place = 0
            for s in range(slots):
                slot = jnp.where(position[s] == k, s, slot)
                place = jnp.where(position[s] == k, places[s], place)
            slot_s[r, k] = slot
            index_s[r, k] = place

    def arrive(k):
        source = partner(k)
        remote(
            out_buf.at[source], land.at[source], dat_send.at[source], dat_recv.at[source], source
        ).wait_recv()
        stage[rows + source] = land[source]

    @pl.loop(0, n - 1 - slots)
    def _(k):
        arrive(k)

    a_copy.wait()

    for k in range(slots):
        arrive(n - 1 - slots + k)

        for r in range(rows):
            term = jnp.dot(
                a_vm[r, slot_s[r, k]], stage[index_s[r, k]], preferred_element_type=F32
            )
            if k > 0:
                term = term + acc[r]
            acc[r] = term
            if k == slots - 1:
                high, low = split(term)
                square = lax.dot_general(
                    high, jnp.concatenate([high, low], axis=1), (((0,), (0,)), ((), ())),
                    preferred_element_type=F32,
                )
                total = square if r == 0 else total + square

    image_copy = pltpu.make_async_copy(acc, image_hbm, image_sem)
    image_copy.start()
    cross = total[:, cols:]
    part[...] = total[:, :cols] + cross + cross.T

    @pl.loop(0, m, unroll=unroll)
    def _(t):
        @pl.when(t != me)
        def _():
            remote(
                part.at[pl.ds(t * share, share)], gram_in.at[me], rs_send.at[t], rs_recv.at[me], t
            ).start()

    @pl.loop(0, n - 1, unroll=unroll)
    def _(k):
        target = (me + k + 1) % n
        remote(
            req_out.at[target], req_in.at[me], req_send.at[target], req_recv.at[me], target
        ).wait_send()
        remote(
            out_buf.at[target], land.at[me], dat_send.at[target], dat_recv.at[me], target
        ).wait_send()

    image_copy.wait()

    @pl.when(me < m)
    def _():
        gram_in[me] = part[pl.ds(pl.multiple_of(me * share, share), share), :]

        @pl.loop(0, n - 1, unroll=unroll)
        def _(k):
            source = (me + k + 1) % n
            remote(
                part.at[pl.ds(0, share)], gram_in.at[source], rs_send.at[0], rs_recv.at[source], source
            ).wait_recv()

        chunk[...] = jnp.sum(gram_in[...], axis=0)

        @pl.loop(0, n - 1, unroll=unroll)
        def _(k):
            target = (me + k + 1) % n
            remote(
                chunk, gram_out.at[pl.ds(me * share, share)], ag_send.at[target], ag_recv.at[me], target
            ).start()

        gram_out[pl.ds(pl.multiple_of(me * share, share), share), :] = chunk[...]

    @pl.loop(0, m, unroll=unroll)
    def _(t):
        @pl.when(t != me)
        def _():
            remote(
                part.at[pl.ds(t * share, share)], gram_in.at[me], rs_send.at[t], rs_recv.at[me], t
            ).wait_send()

    @pl.loop(0, m, unroll=unroll)
    def _(t):
        @pl.when(t != me)
        def _():
            remote(
                chunk, gram_out.at[pl.ds(t * share, share)], ag_send.at[t], ag_recv.at[t], t
            ).wait_recv()

    @pl.when(me < m)
    def _():
        @pl.loop(0, n - 1, unroll=unroll)
        def _(k):
            target = (me + k + 1) % n
            remote(
                chunk, gram_out.at[pl.ds(me * share, share)], ag_send.at[target], ag_recv.at[me], target
            ).wait_send()


def product_and_gram(a_blocks, own_blocks, pattern):
    n = lax.axis_size("rows")
    rows, slots, size, unused = a_blocks.shape
    cols = own_blocks.shape[2]
    share = 8
    m = cols // share
    assert n >= m and n > slots and n & (n - 1) == 0
    vmem = pl.BlockSpec(memory_space=pltpu.VMEM)
    dma = pltpu.SemaphoreType.DMA
    return pl.pallas_call(
        functools.partial(product_kernel, n, m),
        out_shape=(
            jax.ShapeDtypeStruct((rows, size, cols), F32),
            jax.ShapeDtypeStruct((cols, cols), F32),
        ),
        in_specs=[
            pl.BlockSpec(memory_space=pltpu.HBM),
            pl.BlockSpec(memory_space=pltpu.HBM),
            pl.BlockSpec(memory_space=pltpu.HBM),
        ],
        out_specs=(pl.BlockSpec(memory_space=pltpu.HBM), vmem),
        scratch_shapes=[
            pltpu.VMEM((rows, slots), jnp.int32),
            pltpu.SMEM((rows, slots), jnp.int32),
            pltpu.VMEM(a_blocks.shape, BF16),
            pltpu.VMEM((n, 1, 128), jnp.int32),
            pltpu.VMEM((n, 1, 128), jnp.int32),
            pltpu.VMEM((n, size, cols), BF16),
            pltpu.VMEM((n, size, cols), BF16),
            pltpu.VMEM((rows + n, size, cols), BF16),
            pltpu.VMEM((rows, size, cols), F32),
            pltpu.VMEM((cols, cols), F32),
            pltpu.VMEM((n, share, cols), F32),
            pltpu.VMEM((share, cols), F32),
            pltpu.SMEM((rows, slots), jnp.int32),
            pltpu.SMEM((rows, slots), jnp.int32),
            dma, dma, dma, dma, dma,
            dma((n,)), dma((n,)), dma((n,)), dma((n,)),
            dma((n,)), dma((n,)), dma((n,)), dma((n,)),
        ],
        compiler_params=pltpu.CompilerParams(
            collective_id=0, has_side_effects=True, vmem_limit_bytes=64 * 1024 * 1024
        ),
        name="product_and_gram",
    )(a_blocks, own_blocks, pattern)


def lanes(x, width):
    return jnp.broadcast_to(x, (x.shape[0], width))


def sublanes(x, i):
    return jnp.broadcast_to(x[i:i + 1], x.shape)


def three(x):
    high = x.astype(BF16).astype(F32)
    rest = x - high
    middle = rest.astype(BF16).astype(F32)
    return high, middle, rest - middle


def factor_kernel(
    scale, step, gram_hbm, image_hbm, basis_hbm, factor, gram, image, result, gram_sem, in_sem, out_sem
):
    cols = gram.shape[0]
    chunks, size, unused = image.shape
    gram_copy = pltpu.make_async_copy(gram_hbm, gram, gram_sem)
    gram_copy.start()
    image_copy = pltpu.make_async_copy(image_hbm, image, in_sem)
    image_copy.start()
    gram_copy.wait()
    down = lax.broadcasted_iota(jnp.int32, (cols, cols), 0)
    across = lax.broadcasted_iota(jnp.int32, (cols, cols), 1)
    rest = jnp.concatenate([gram[...] * scale, jnp.where(down == across, 1.0, 0.0)], axis=1)
    halves = step // 8
    sub = lax.broadcasted_iota(jnp.int32, (8, cols), 0)
    uppers = []
    lowers = []
    for start in range(0, cols, step):
        panel = [rest[8 * h:8 * h + 8] for h in range(halves)]
        column = [
            [lanes(panel[h][:, start + l:start + l + 1], cols) for h in range(halves)]
            for l in range(step)
        ]
        left = [p[:, :cols] for p in panel]
        right = [p[:, cols:] for p in panel]
        pivots = [jnp.ones((8, cols), F32) for h in range(halves)]
        for k in range(step):
            h0, i0 = divmod(k, 8)
            pivot = sublanes(column[k][h0], i0)
            pivots[h0] = jnp.where(sub == i0, pivot, pivots[h0])
            inverse = 1.0 / pivot
            below = [
                jnp.where(sub > i0, column[k][h], 0.0) if h == h0 else column[k][h]
                for h in range(h0, halves)
            ]
            for l in range(k + 1, step):
                weight = sublanes(column[l][h0], i0) * inverse
                for h in range(h0, halves):
                    column[l][h] = column[l][h] - below[h - h0] * weight
            top_left = sublanes(left[h0], i0) * inverse
            top_right = sublanes(right[h0], i0) * inverse
            for h in range(h0, halves):
                left[h] = left[h] - below[h - h0] * top_left
                right[h] = right[h] - below[h - h0] * top_right
        roots = [lax.rsqrt(p) for p in pivots]
        new_left = jnp.concatenate([l * r for l, r in zip(left, roots)], axis=0)
        new_right = jnp.concatenate([l * r for l, r in zip(right, roots)], axis=0)
        uppers.append(new_left)
        lowers.append(new_right)
        if start + step < cols:
            a1, a2, a3 = three(new_left)
            b1, b2, b3 = three(new_right)
            lhs = jnp.concatenate([a1, a1, a2, a2, a1, a3], axis=0).astype(BF16)
            rhs = jnp.concatenate(
                [
                    jnp.concatenate([a1, a2, a1, a2, a3, a1], axis=0),
                    jnp.concatenate([b1, b2, b1, b2, b3, b1], axis=0),
                ],
                axis=1,
            ).astype(BF16)
            change = lax.dot_general(
                lhs, rhs, (((0,), (0,)), ((), ())), preferred_element_type=F32
            )
            rest = rest[step:] - change[start + step:]
    upper = jnp.concatenate(uppers, axis=0)
    lower = jnp.concatenate(lowers, axis=0)
    factor[...] = jnp.where(across >= down, upper, 0.0)
    high, low = split(lower)
    both = jnp.concatenate([high, high], axis=1)
    image_copy.wait()
    turned = (((1,), (1,)), ((), ()))
    for c in range(chunks):
        x_high, x_low = split(image[c])
        result[c] = lax.dot_general(
            jnp.concatenate([x_high, x_low], axis=1), both, turned, preferred_element_type=F32
        ) + lax.dot_general(x_high, low, turned, preferred_element_type=F32)
        pltpu.make_async_copy(result.at[c], basis_hbm.at[c], out_sem.at[c]).start()
    for c in range(chunks):
        pltpu.make_async_copy(result.at[c], basis_hbm.at[c], out_sem.at[c]).wait()


def factor_and_basis(gram, image, nodes):
    vmem = pl.BlockSpec(memory_space=pltpu.VMEM)
    dma = pltpu.SemaphoreType.DMA
    return pl.pallas_call(
        functools.partial(factor_kernel, 1.0 / nodes, STEP),
        out_shape=(
            jax.ShapeDtypeStruct(image.shape, F32),
            jax.ShapeDtypeStruct(gram.shape, F32),
        ),
        in_specs=[pl.BlockSpec(memory_space=pltpu.HBM)] * 2,
        out_specs=(pl.BlockSpec(memory_space=pltpu.HBM), vmem),
        scratch_shapes=[
            pltpu.VMEM(gram.shape, F32), pltpu.VMEM(image.shape, F32), pltpu.VMEM(image.shape, F32),
            dma, dma, dma((image.shape[0],)),
        ],
        compiler_params=pltpu.CompilerParams(vmem_limit_bytes=64 * 1024 * 1024),
        name="factor_and_basis",
    )(gram, image)


def shards(a_blocks, basis_in, pattern):
    n = lax.axis_size("rows")
    rows, slots, size, unused = a_blocks.shape
    cols = basis_in.shape[1]
    image, gram = product_and_gram(a_blocks, basis_in.reshape(rows, size, cols), pattern)
    basis_out, factor = factor_and_basis(gram, image, n * rows * size)
    return (basis_out.reshape(rows * size, cols), factor)


def solution(mesh):
    placed = (
        P(("groups", "rows"), None, None, None),
        P(("groups", "rows"), None),
        P(("groups", "rows"), None),
    )
    return jax.shard_map(
        shards,
        mesh=mesh,
        in_specs=placed,
        out_specs=(P(("groups", "rows"), None), P("groups", None)),
        check_vma=False,
    )
```

```python
import functools
import jax
import jax.numpy as jnp
from jax import lax
from jax.experimental import pallas as pl
from jax.experimental.pallas import tpu as pltpu
from jax.sharding import PartitionSpec as P

MESH = pl.DeviceIdType.MESH
F32 = jnp.float32
BF16 = jnp.bfloat16
STEP = 16


def split(x):
    hi = x.astype(BF16)
    lo = (x - hi.astype(F32)).astype(BF16)
    return hi, lo


def product_kernel(
    n, m, a_hbm, basis_hbm, pat_hbm, image_hbm, gram_out,
    pat_v, pat_s, a_vm, req_out, req_in, out_buf, land, stage, acc, part, gram_in, chunk,
    slot_s, index_s,
    a_sem, basis_sem, pat_v_sem, pat_s_sem, image_sem, req_send, req_recv, dat_send, dat_recv, rs_send, rs_recv, ag_send, ag_recv,
):
    me = lax.axis_index("rows")
    rows, slots = pat_s.shape
    cols = part.shape[1]
    share = chunk.shape[0]

    def partner(k):
        d = k + 1
        other = me + d
        bit = 1
        while bit < n:
            other = other - 2 * bit * ((me // bit) % 2) * ((d // bit) % 2)
            bit *= 2
        return other

    def remote(src, dst, send, recv, target):
        return pltpu.make_async_remote_copy(
            src_ref=src, dst_ref=dst, send_sem=send, recv_sem=recv,
            device_id={"rows": target}, device_id_type=MESH,
        )

    unroll = n <= 16
    pat_v_copy = pltpu.make_async_copy(pat_hbm, pat_v, pat_v_sem)
    pat_v_copy.start()
    pat_s_copy = pltpu.make_async_copy(pat_hbm, pat_s, pat_s_sem)
    pat_s_copy.start()
    basis_copy = pltpu.make_async_copy(basis_hbm, stage.at[pl.ds(0, rows)], basis_sem)
    basis_copy.start()
    barrier = pltpu.get_barrier_semaphore()

    @pl.loop(0, n - 1, unroll=unroll)
    def _(k):
        pl.semaphore_signal(
            barrier, inc=1, device_id={"rows": (me + k + 1) % n}, device_id_type=MESH
        )

    a_copy = pltpu.make_async_copy(a_hbm, a_vm, a_sem)
    a_copy.start()
    pat_v_copy.wait()
    pattern = pat_v[...][None]
    owner_ids = lax.broadcasted_iota(jnp.int32, (n, rows, slots), 0)
    local = pattern - owner_ids * rows
    named = jnp.where((local >= 0) & (local < rows), local, 0)
    asked = jnp.max(jnp.max(named, axis=2, keepdims=True), axis=1, keepdims=True)
    req_out[...] = jnp.broadcast_to(asked, req_out.shape)
    basis_copy.wait()
    pat_s_copy.wait()
    pl.semaphore_wait(barrier, n - 1)

    @pl.loop(0, n - 1, unroll=unroll)
    def _(k):
        target = partner(k)
        remote(
            req_out.at[target], req_in.at[me], req_send.at[target], req_recv.at[me], target
        ).start()

    @pl.loop(0, n - 1, unroll=unroll)
    def _(k):
        target = partner(k)
        remote(
            req_out.at[target], req_in.at[target], req_send.at[target], req_recv.at[target], target
        ).wait_recv()
        wanted = req_in[target][0, 0]
        out_buf[target] = stage[wanted]
        remote(
            out_buf.at[target], land.at[me], dat_send.at[target], dat_recv.at[me], target
        ).start()

    @pl.loop(0, rows)
    def _(r):
        keys = []
        places = []
        for s in range(slots):
            col = pat_s[r, s]
            owner = col // rows
            rank = jnp.bitwise_xor(owner, me)
            keys.append(rank * slots + s)
            places.append(jnp.where(owner == me, col - owner * rows, rows + owner))
        position = []
        for s in range(slots):
            count = 0
            for t in range(slots):
                if t != s:
                    count = count + jnp.where(keys[t] < keys[s], 1, 0)
            position.append(count)
        for k in range(slots):
            slot = 0
            place = 0
            for s in range(slots):
                slot = jnp.where(position[s] == k, s, slot)
                place = jnp.where(position[s] == k, places[s], place)
            slot_s[r, k] = slot
            index_s[r, k] = place

    def arrive(k):
        source = partner(k)
        remote(
            out_buf.at[source], land.at[source], dat_send.at[source], dat_recv.at[source], source
        ).wait_recv()
        stage[rows + source] = land[source]

    @pl.loop(0, n - 1 - slots)
    def _(k):
        arrive(k)

    a_copy.wait()

    for k in range(1, slots, 2):
        arrive(n - 2 - slots + k)
        arrive(n - 1 - slots + k)

        for r in range(rows):
            term = jnp.dot(
                a_vm[r, slot_s[r, k - 1]], stage[index_s[r, k - 1]], preferred_element_type=F32
            ) + jnp.dot(
                a_vm[r, slot_s[r, k]], stage[index_s[r, k]], preferred_element_type=F32
            )
            if k > 1:
                term = term + acc[r]
            acc[r] = term
            if k == slots - 1:
                high, low = split(term)
                square = lax.dot_general(
                    high, jnp.concatenate([high, low], axis=1), (((0,), (0,)), ((), ())),
                    preferred_element_type=F32,
                )
                total = square if r == 0 else total + square

    image_copy = pltpu.make_async_copy(acc, image_hbm, image_sem)
    image_copy.start()
    cross = total[:, cols:]
    part[...] = total[:, :cols] + cross + cross.T

    @pl.loop(0, m, unroll=unroll)
    def _(t):
        @pl.when(t != me)
        def _():
            remote(
                part.at[pl.ds(t * share, share)], gram_in.at[me], rs_send.at[t], rs_recv.at[me], t
            ).start()

    @pl.loop(0, n - 1, unroll=unroll)
    def _(k):
        target = (me + k + 1) % n
        remote(
            req_out.at[target], req_in.at[me], req_send.at[target], req_recv.at[me], target
        ).wait_send()
        remote(
            out_buf.at[target], land.at[me], dat_send.at[target], dat_recv.at[me], target
        ).wait_send()

    image_copy.wait()

    @pl.when(me < m)
    def _():
        gram_in[me] = part[pl.ds(pl.multiple_of(me * share, share), share), :]

        @pl.loop(0, n - 1, unroll=unroll)
        def _(k):
            source = (me + k + 1) % n
            remote(
                part.at[pl.ds(0, share)], gram_in.at[source], rs_send.at[0], rs_recv.at[source], source
            ).wait_recv()

        chunk[...] = jnp.sum(gram_in[...], axis=0)

        @pl.loop(0, n - 1, unroll=unroll)
        def _(k):
            target = (me + k + 1) % n
            remote(
                chunk, gram_out.at[pl.ds(me * share, share)], ag_send.at[target], ag_recv.at[me], target
            ).start()

        gram_out[pl.ds(pl.multiple_of(me * share, share), share), :] = chunk[...]

    @pl.loop(0, m, unroll=unroll)
    def _(t):
        @pl.when(t != me)
        def _():
            remote(
                part.at[pl.ds(t * share, share)], gram_in.at[me], rs_send.at[t], rs_recv.at[me], t
            ).wait_send()

    @pl.loop(0, m, unroll=unroll)
    def _(t):
        @pl.when(t != me)
        def _():
            remote(
                chunk, gram_out.at[pl.ds(t * share, share)], ag_send.at[t], ag_recv.at[t], t
            ).wait_recv()

    @pl.when(me < m)
    def _():
        @pl.loop(0, n - 1, unroll=unroll)
        def _(k):
            target = (me + k + 1) % n
            remote(
                chunk, gram_out.at[pl.ds(me * share, share)], ag_send.at[target], ag_recv.at[me], target
            ).wait_send()


def product_and_gram(a_blocks, own_blocks, pattern):
    n = lax.axis_size("rows")
    rows, slots, size, unused = a_blocks.shape
    cols = own_blocks.shape[2]
    share = 8
    m = cols // share
    assert n >= m and n > slots and n & (n - 1) == 0 and slots % 2 == 0
    vmem = pl.BlockSpec(memory_space=pltpu.VMEM)
    dma = pltpu.SemaphoreType.DMA
    return pl.pallas_call(
        functools.partial(product_kernel, n, m),
        out_shape=(
            jax.ShapeDtypeStruct((rows, size, cols), F32),
            jax.ShapeDtypeStruct((cols, cols), F32),
        ),
        in_specs=[
            pl.BlockSpec(memory_space=pltpu.HBM),
            pl.BlockSpec(memory_space=pltpu.HBM),
            pl.BlockSpec(memory_space=pltpu.HBM),
        ],
        out_specs=(pl.BlockSpec(memory_space=pltpu.HBM), vmem),
        scratch_shapes=[
            pltpu.VMEM((rows, slots), jnp.int32),
            pltpu.SMEM((rows, slots), jnp.int32),
            pltpu.VMEM(a_blocks.shape, BF16),
            pltpu.VMEM((n, 1, 128), jnp.int32),
            pltpu.VMEM((n, 1, 128), jnp.int32),
            pltpu.VMEM((n, size, cols), BF16),
            pltpu.VMEM((n, size, cols), BF16),
            pltpu.VMEM((rows + n, size, cols), BF16),
            pltpu.VMEM((rows, size, cols), F32),
            pltpu.VMEM((cols, cols), F32),
            pltpu.VMEM((n, share, cols), F32),
            pltpu.VMEM((share, cols), F32),
            pltpu.SMEM((rows, slots), jnp.int32),
            pltpu.SMEM((rows, slots), jnp.int32),
            dma, dma, dma, dma, dma,
            dma((n,)), dma((n,)), dma((n,)), dma((n,)),
            dma((n,)), dma((n,)), dma((n,)), dma((n,)),
        ],
        compiler_params=pltpu.CompilerParams(
            collective_id=0, has_side_effects=True, vmem_limit_bytes=64 * 1024 * 1024
        ),
        name="product_and_gram",
    )(a_blocks, own_blocks, pattern)


def lanes(x, width):
    return jnp.broadcast_to(x, (x.shape[0], width))


def sublanes(x, i):
    return jnp.broadcast_to(x[i:i + 1], x.shape)


def three(x):
    high = x.astype(BF16).astype(F32)
    rest = x - high
    middle = rest.astype(BF16).astype(F32)
    return high, middle, rest - middle


def factor_kernel(
    scale, step, gram_hbm, image_hbm, basis_hbm, factor, gram, image, result, gram_sem, in_sem, out_sem
):
    cols = gram.shape[0]
    chunks, size, unused = image.shape
    gram_copy = pltpu.make_async_copy(gram_hbm, gram, gram_sem)
    gram_copy.start()
    image_copy = pltpu.make_async_copy(image_hbm, image, in_sem)
    image_copy.start()
    gram_copy.wait()
    down = lax.broadcasted_iota(jnp.int32, (cols, cols), 0)
    across = lax.broadcasted_iota(jnp.int32, (cols, cols), 1)
    rest = jnp.concatenate([gram[...] * scale, jnp.where(down == across, 1.0, 0.0)], axis=1)
    halves = step // 8
    sub = lax.broadcasted_iota(jnp.int32, (8, cols), 0)
    uppers = []
    lowers = []
    for start in range(0, cols, step):
        panel = [rest[8 * h:8 * h + 8] for h in range(halves)]
        column = [
            [lanes(panel[h][:, start + l:start + l + 1], cols) for h in range(halves)]
            for l in range(step)
        ]
        left = [p[:, :cols] for p in panel]
        right = [p[:, cols:] for p in panel]
        pivots = [jnp.ones((8, cols), F32) for h in range(halves)]
        for k in range(step):
            h0, i0 = divmod(k, 8)
            pivot = sublanes(column[k][h0], i0)
            pivots[h0] = jnp.where(sub == i0, pivot, pivots[h0])
            inverse = 1.0 / pivot
            below = [
                jnp.where(sub > i0, column[k][h], 0.0) if h == h0 else column[k][h]
                for h in range(h0, halves)
            ]
            for l in range(k + 1, step):
                weight = sublanes(column[l][h0], i0) * inverse
                for h in range(h0, halves):
                    column[l][h] = column[l][h] - below[h - h0] * weight
            top_left = sublanes(left[h0], i0) * inverse
            top_right = sublanes(right[h0], i0) * inverse
            for h in range(h0, halves):
                left[h] = left[h] - below[h - h0] * top_left
                right[h] = right[h] - below[h - h0] * top_right
        roots = [lax.rsqrt(p) for p in pivots]
        new_left = jnp.concatenate([l * r for l, r in zip(left, roots)], axis=0)
        new_right = jnp.concatenate([l * r for l, r in zip(right, roots)], axis=0)
        uppers.append(new_left)
        lowers.append(new_right)
        if start + step < cols:
            a1, a2, a3 = three(new_left)
            b1, b2, b3 = three(new_right)
            lhs = jnp.concatenate([a1, a1, a2, a2, a1, a3], axis=0).astype(BF16)
            rhs = jnp.concatenate(
                [
                    jnp.concatenate([a1, a2, a1, a2, a3, a1], axis=0),
                    jnp.concatenate([b1, b2, b1, b2, b3, b1], axis=0),
                ],
                axis=1,
            ).astype(BF16)
            change = lax.dot_general(
                lhs, rhs, (((0,), (0,)), ((), ())), preferred_element_type=F32
            )
            rest = rest[step:] - change[start + step:]
    upper = jnp.concatenate(uppers, axis=0)
    lower = jnp.concatenate(lowers, axis=0)
    factor[...] = jnp.where(across >= down, upper, 0.0)
    high, low = split(lower)
    both = jnp.concatenate([high, high], axis=1)
    image_copy.wait()
    turned = (((1,), (1,)), ((), ()))
    for c in range(chunks):
        x_high, x_low = split(image[c])
        result[c] = lax.dot_general(
            jnp.concatenate([x_high, x_low], axis=1), both, turned, preferred_element_type=F32
        ) + lax.dot_general(x_high, low, turned, preferred_element_type=F32)
        pltpu.make_async_copy(result.at[c], basis_hbm.at[c], out_sem.at[c]).start()
    for c in range(chunks):
        pltpu.make_async_copy(result.at[c], basis_hbm.at[c], out_sem.at[c]).wait()


def factor_and_basis(gram, image, nodes):
    vmem = pl.BlockSpec(memory_space=pltpu.VMEM)
    dma = pltpu.SemaphoreType.DMA
    return pl.pallas_call(
        functools.partial(factor_kernel, 1.0 / nodes, STEP),
        out_shape=(
            jax.ShapeDtypeStruct(image.shape, F32),
            jax.ShapeDtypeStruct(gram.shape, F32),
        ),
        in_specs=[pl.BlockSpec(memory_space=pltpu.HBM)] * 2,
        out_specs=(pl.BlockSpec(memory_space=pltpu.HBM), vmem),
        scratch_shapes=[
            pltpu.VMEM(gram.shape, F32), pltpu.VMEM(image.shape, F32), pltpu.VMEM(image.shape, F32),
            dma, dma, dma((image.shape[0],)),
        ],
        compiler_params=pltpu.CompilerParams(vmem_limit_bytes=64 * 1024 * 1024),
        name="factor_and_basis",
    )(gram, image)


def shards(a_blocks, basis_in, pattern):
    n = lax.axis_size("rows")
    rows, slots, size, unused = a_blocks.shape
    cols = basis_in.shape[1]
    image, gram = product_and_gram(a_blocks, basis_in.reshape(rows, size, cols), pattern)
    basis_out, factor = factor_and_basis(gram, image, n * rows * size)
    return (basis_out.reshape(rows * size, cols), factor)


def solution(mesh):
    placed = (
        P(("groups", "rows"), None, None, None),
        P(("groups", "rows"), None),
        P(("groups", "rows"), None),
    )
    return jax.shard_map(
        shards,
        mesh=mesh,
        in_specs=placed,
        out_specs=(P(("groups", "rows"), None), P("groups", None)),
        check_vma=False,
    )
```
